32 devices in a mesh: groups: 2 (over x), dp: 8 (over z, y), layer: 2 (over core).
Axes of the slice: x: 2, y: 2, z: 4, core: 2. Of those that a mesh axis runs over, the one named last changes fastest.
Arguments:
- store: float32 [2, 8192, 4096], P('layer', ('groups', 'dp')), parts along dimension 1, may hold values from -0.09375 to 0.09375
- queries: float32 [2, 256, 4096], P('layer', 'dp'), may hold values from -6 to 6
- second_moment: float32 [2, 4096], P('layer'), may hold values from 0.25 to 4
- layer_rate: float32 [2], P('layer'), may hold values from 0.5 to 2
- query_task: int32 [256, 1], replicated, may hold values from 0 to 15
Outputs:
- best: float32 [16, 8192], P(None, ('groups', 'dp')), parts along dimension 1
The draws below stay inside these ranges and needn't reach their ends.
There are 2 independent parts, one for each index of `groups`. The reference program is written for one: setup_inputs(seed, part) draws one part's arguments, and reference() takes and returns one part's arrays. A program takes and returns all parts, laid end to end along the dimension named above; an argument that names none is the same for every part. Nothing has to cross between parts.
Inputs may be any that keep to these rules, and one draw needn't show every extreme that they name: `query_task`: every task 0 to 15 is named by some query.
All inputs are finite; a program needn't handle non-finite values.
Results may differ from the reference program's by a relative error of at most 0.0018.
Values may be sent and summed in bfloat16 or wider, within the bound.
A program may use at most 128 MiB of HBM per device.

```python
import math
import jax
import jax.numpy as jnp
from jax import lax

K = 4096
TASKS = 16
LAYERS = 2
EXAMPLES = 4096
NQ = 256


def level_of(stream_key, dims, cuts, smallest, high):
    level, own = 1.0, jax.random.fold_in(stream_key, 6)
    for position, blocks in cuts:
        heights = jnp.exp(jax.random.uniform(jax.random.fold_in(own, position), (blocks,), jnp.float32, smallest / len(cuts), high / len(cuts)))
        level = level * jnp.repeat(heights, dims[position] // blocks).reshape([-1 if axis == position else 1 for axis in range(len(dims))])
    return level


def choose_distinct(key, rows, number_of, top, lift):
    sequence = jax.random.permutation(jax.random.fold_in(key, 1), number_of)
    favour = sequence
    for power in range(3):
        favour = favour * favour // number_of
    favour = favour * lift // number_of
    lots = jax.random.randint(jax.random.fold_in(key, 2), (rows, number_of), 0, 4096) + favour
    fixed_rows = jax.random.permutation(jax.random.fold_in(key, 3), rows)[jnp.arange(number_of) % rows]
    lots = jnp.where(jnp.arange(rows)[:, None] == fixed_rows[None, :], 1 << 14, lots)
    score = lots * number_of + jnp.arange(number_of)
    return lax.top_k(score.astype(jnp.int32), top)[1].astype(jnp.int32)


def normal_values(key, extent, deviation, bound, split=(), held_as=jnp.bfloat16):
    array = deviation * jax.random.normal(key, extent, jnp.float32)
    if split:
        array = array * level_of(key, extent, split, -0.22, 0.18)
    return jnp.clip(array, -bound, bound).astype(held_as)


def setup_inputs(seed: int = 0, part: int = 0) -> dict:
    key_list = jax.random.split(jax.random.key(seed), 6)
    own_keys = jax.random.split(jax.random.fold_in(key_list[5], part), 6)
    store = normal_values(own_keys[0], (LAYERS, EXAMPLES, K), (K ** -0.5), 0.09375, ((0, 2), (1, 8)), jnp.float32)
    queries = normal_values(key_list[1], (LAYERS, NQ, K), 1.0, 6.0, ((0, 2), (1, 8)), jnp.float32)
    second_moment = jnp.clip(jnp.exp(math.log(4.0) - 2.7725887 * jax.random.uniform(key_list[2], (LAYERS, K), jnp.float32) ** level_of(key_list[2], (LAYERS, K), ((0, 2),), -0.2, 0.2)), 0.25, 4.0)
    layer_rate = jnp.clip(jnp.exp(math.log(2.0) - 1.3862944 * jax.random.uniform(key_list[3], (LAYERS,), jnp.float32) ** level_of(key_list[3], (LAYERS,), ((0, 2),), -0.2, 0.2)), 0.5, 2.0)
    query_task = choose_distinct(key_list[4], NQ, TASKS, 1, 0)
    return {"store": store, "queries": queries, "second_moment": second_moment, "layer_rate": layer_rate, "query_task": query_task}


def reference(store, queries, second_moment, layer_rate, query_task):
    scores = jnp.zeros((queries.shape[1], store.shape[1]), jnp.float32)
    for level in range(LAYERS):
        factor = layer_rate[level] * lax.rsqrt(second_moment[level])
        precond = (queries[level] * factor[None, :]).astype(jnp.bfloat16)
        scores = scores + lax.dot_general(precond.astype(jnp.float32), store[level], (((1,), (1,)), ((), ())), precision=lax.Precision.HIGHEST, preferred_element_type=jnp.float32)
    task_ids = jnp.arange(TASKS, dtype=jnp.int32)
    masks = query_task[:, 0][None, :] == task_ids[:, None]

    def peak(member):
        return lax.optimization_barrier(jnp.max(jnp.where(member[:, None], scores, -jnp.inf), axis=0))
    return lax.map(peak, masks)
```

```python
import functools

import jax
import jax.numpy as jnp
from jax import lax
from jax.experimental import pallas as pl
from jax.experimental.pallas import tpu as pltpu
from jax.sharding import PartitionSpec as P

TASKS = 16
QUARTERS = 4
MESH = pl.DeviceIdType.MESH


def kernel(
    length,
    store_ref,
    query_ref,
    moment_ref,
    rate_ref,
    task_ref,
    out_ref,
    raw,
    high,
    low,
    own,
    rows,
    acc,
    other,
    best,
    store_sem,
    query_sem,
    recv_sem,
    line_sem,
    plane_sem,
    pair_send,
    pair_recv,
):
    x = lax.axis_index("groups")
    dp = lax.axis_index("dp")
    core = lax.axis_index("layer")
    z, y = dp // 2, dp % 2
    parity = (x + y) % 2
    mine, theirs = 2 * parity, 2 * (1 - parity)
    width = raw.shape[2]
    to_x = {"groups": 1 - x}
    to_y = {"dp": z * 2 + 1 - y}
    to_core = {"layer": 1 - core}
    to_line = ({"dp": dp - 2}, {"dp": dp + 2})
    has_line = (z > 0, z < length - 1)

    get_query = pltpu.make_async_copy(query_ref.at[0], own, query_sem)
    get_query.start()
    get_store = [
        pltpu.make_async_copy(
            store_ref.at[0, :, pl.ds(i * width, width)], raw.at[i], store_sem.at[i]
        )
        for i in range(QUARTERS)
    ]
    for copy in get_store:
        copy.start()

    barrier = pltpu.get_barrier_semaphore()
    for peer in (to_x, to_y, to_core):
        pl.semaphore_signal(barrier, inc=1, device_id=peer, device_id_type=MESH)
    for way in range(2):

        @pl.when(has_line[way])
        def _():
            pl.semaphore_signal(
                barrier, inc=1, device_id=to_line[way], device_id_type=MESH
            )

    def chunk_copy(shard, quarter, send_sem, peer):
        return pltpu.make_async_remote_copy(
            src_ref=rows.at[shard, quarter],
            dst_ref=rows.at[shard, quarter],
            send_sem=send_sem,
            recv_sem=recv_sem.at[shard, quarter],
            device_id=peer,
            device_id_type=MESH,
        )

    def line(shard, quarter, way):
        return chunk_copy(shard, quarter, line_sem.at[shard, quarter, way], to_line[way])

    def plane(shard, quarter, peer):
        return chunk_copy(shard, quarter, plane_sem.at[shard, quarter], peer)

    def arrived(shard, quarter):
        plane(shard, quarter, to_x).wait_recv()

    def pair(block):
        return pltpu.make_async_remote_copy(
            src_ref=acc.at[block],
            dst_ref=other.at[block],
            send_sem=pair_send.at[block],
            recv_sem=pair_recv.at[block],
            device_id=to_core,
            device_id_type=MESH,
        )

    def piece(block, quarter):
        count = rows.shape[2]
        left = jnp.concatenate(
            [rows[2 * block, quarter], rows[2 * block + 1, quarter]], axis=0
        )
        dims = (((1,), (1,)), ((), ()))
        acc[block] += lax.dot_general(
            left, high[quarter], dims, preferred_element_type=jnp.float32
        ) + lax.dot_general(
            left, low[quarter], dims, preferred_element_type=jnp.float32
        )

    def convert(i):
        get_store[i].wait()
        step = 64

        def body(r, _):
            at = pl.ds(pl.multiple_of(r * step, step), step)
            value = raw[i, at, :]
            top = value.astype(jnp.bfloat16)
            high[i, at, :] = top
            low[i, at, :] = (value - top.astype(jnp.float32)).astype(jnp.bfloat16)
            return 0

        lax.fori_loop(0, raw.shape[1] // step, body, 0)

    def peak(block):
        pair(block).wait_recv()
        count = acc.shape[1]
        scores = acc[block] + other[block]
        tasks = task_ref[pl.ds(pl.multiple_of(block * count, count), count), :]
        tasks = jnp.broadcast_to(tasks, scores.shape)
        for t in range(TASKS):
            value = jnp.where(tasks == t, scores, -jnp.inf)
            value = jnp.max(value.reshape(count // 8, 8, scores.shape[1]), axis=0)
            best[t] = jnp.maximum(best[t], value)

    def finish(block, quarter):
        piece(block, quarter)
        pair(block).start()

    get_query.wait()
    me, mate = dp, z * 2 + 1 - y
    for i in range(QUARTERS):
        at = pl.ds(i * width, width)
        factor = rate_ref[0] * lax.rsqrt(moment_ref[:, at])
        rows[me, i] = (own[:, at] * factor).astype(jnp.bfloat16)

    waits = 3 + jnp.where(z > 0, 1, 0) + jnp.where(z < length - 1, 1, 0)
    pl.semaphore_wait(barrier, waits)

    for j in range(2):
        plane(me, theirs + j, to_y).start()
        for way in range(2):

            @pl.when(has_line[way])
            def _():
                line(me, mine + j, way).start()

    acc[...] = jnp.zeros_like(acc)
    best[...] = jnp.full_like(best, -jnp.inf)
    for j in range(2):
        convert(j)
        arrived(mate, mine + j)
        for way in range(2):

            @pl.when(has_line[way])
            def _():
                line(mate, mine + j, way).start()

        plane(mate, mine + j, to_x).start()
    convert(2)
    convert(3)
    piece(z, mine)
    piece(z, mine + 1)
    arrived(mate, theirs)
    piece(z, theirs)
    arrived(mate, theirs + 1)
    finish(z, theirs + 1)

    def source(far, way):
        return z - far if way == 0 else z + far

    def valid(src):
        return (src >= 0) & (src < length)

    def over_ways(far, action):
        def body(way, _):
            src = z + (2 * way - 1) * far

            @pl.when(valid(src))
            def _():
                action(src)

            return 0

        lax.fori_loop(0, 2, body, 0)

    def last_piece(src):
        arrived(2 * src, theirs + 1)
        arrived(2 * src + 1, theirs + 1)
        finish(src, theirs + 1)

    def round_of(far, _):
        for j in range(2):
            for side in range(2):
                for way in range(2):
                    src = source(far, way)
                    shard = 2 * src + side

                    @pl.when(valid(src))
                    def _():
                        arrived(shard, mine + j)

                        @pl.when(has_line[1 - way])
                        def _():
                            line(shard, mine + j, 1 - way).start()

                        plane(shard, mine + j, to_x if j == 0 else to_y).start()

            over_ways(far, lambda src: piece(src, mine + j))
            if j == 0:

                @pl.when(far > 1)
                def _():
                    over_ways(far - 1, last_piece)
            else:

                def early_piece(src):
                    arrived(2 * src, theirs)
                    arrived(2 * src + 1, theirs)
                    piece(src, theirs)

                over_ways(far, early_piece)

                @pl.when(far == 1)
                def _():
                    peak(z)

                @pl.when(far > 1)
                def _():
                    over_ways(far - 1, peak)

        return 0

    lax.fori_loop(1, length, round_of, 0)
    over_ways(length - 1, last_piece)
    over_ways(length - 1, peak)

    for t in range(TASKS):
        out_ref[pl.ds(t, 1), :] = jnp.max(best[t], axis=0, keepdims=True)

    for j in range(2):
        plane(me, theirs + j, to_y).wait_send()
        plane(mate, mine + j, to_x).wait_send()
        for way in range(2):

            @pl.when(has_line[way])
            def _():
                line(me, mine + j, way).wait_send()
                line(mate, mine + j, way).wait_send()

    pair(z).wait_send()

    def drain(far, _):
        for way in range(2):
            src = source(far, way)

            @pl.when(valid(src))
            def _():
                pair(src).wait_send()
                for j in range(2):
                    for side in range(2):
                        shard = 2 * src + side
                        plane(shard, mine + j, to_x if j == 0 else to_y).wait_send()

                        @pl.when(has_line[1 - way])
                        def _():
                            line(shard, mine + j, 1 - way).wait_send()

        return 0

    lax.fori_loop(1, length, drain, 0)


def on_device(mesh_dp, store, queries, second_moment, layer_rate, query_task):
    length = mesh_dp // 2
    examples, depth = store.shape[1], store.shape[2]
    each = queries.shape[1]
    width = depth // QUARTERS
    dma, vmem = pltpu.SemaphoreType.DMA, pltpu.VMEM
    return pl.pallas_call(
        functools.partial(kernel, length),
        out_shape=jax.ShapeDtypeStruct((TASKS, examples), jnp.float32),
        in_specs=[
            pl.BlockSpec(memory_space=pl.ANY),
            pl.BlockSpec(memory_space=pl.ANY),
            pl.BlockSpec(memory_space=pltpu.VMEM),
            pl.BlockSpec(memory_space=pltpu.SMEM),
            pl.BlockSpec(memory_space=pltpu.VMEM),
        ],
        out_specs=pl.BlockSpec(memory_space=pltpu.VMEM),
        scratch_shapes=[
            vmem((QUARTERS, examples, width), jnp.float32),
            vmem((QUARTERS, examples, width), jnp.bfloat16),
            vmem((QUARTERS, examples, width), jnp.bfloat16),
            vmem((each, depth), jnp.float32),
            vmem((mesh_dp, QUARTERS, each, width), jnp.bfloat16),
            vmem((length, 2 * each, examples), jnp.float32),
            vmem((length, 2 * each, examples), jnp.float32),
            vmem((TASKS, 8, examples), jnp.float32),
            dma((QUARTERS,)),
            dma,
            dma((mesh_dp, QUARTERS)),
            dma((mesh_dp, QUARTERS, 2)),
            dma((mesh_dp, QUARTERS)),
            dma((length,)),
            dma((length,)),
        ],
        compiler_params=pltpu.CompilerParams(
            collective_id=0, has_side_effects=True, vmem_limit_bytes=56 * 1024 * 1024
        ),
        cost_estimate=pl.CostEstimate(
            flops=4 * each * mesh_dp * examples * depth,
            bytes_accessed=4 * (examples + each) * depth,
            transcendentals=depth,
        ),
    )(store, queries, second_moment, layer_rate, query_task)


def solution(mesh):
    in_specs = (
        P("layer", ("groups", "dp"), None),
        P("layer", "dp", None),
        P("layer", None),
        P("layer"),
        P(),
    )
    out_specs = P(None, ("groups", "dp"))
    return jax.shard_map(
        functools.partial(on_device, mesh.shape["dp"]),
        mesh=mesh,
        in_specs=in_specs,
        out_specs=out_specs,
        check_vma=False,
    )
```

```python
import functools

import jax
import jax.numpy as jnp
from jax import lax
from jax.experimental import pallas as pl
from jax.experimental.pallas import tpu as pltpu
from jax.sharding import PartitionSpec as P

TASKS = 16
QUARTERS = 4
PARTS = 1
LANES = 128
MESH = pl.DeviceIdType.MESH


def kernel(
    length,
    store_ref,
    query_ref,
    moment_ref,
    rate_ref,
    task_ref,
    out_ref,
    raw,
    high,
    low,
    own,
    rows,
    acc,
    other,
    best,
    columns,
    store_sem,
    query_sem,
    recv_sem,
    line_sem,
    plane_sem,
    pair_send,
    pair_recv,
):
    x = lax.axis_index("groups")
    dp = lax.axis_index("dp")
    core = lax.axis_index("layer")
    z, y = dp // 2, dp % 2
    parity = (x + y) % 2
    mine, theirs = 2 * parity, 2 * (1 - parity)
    width = raw.shape[2]
    edge = (z == 0) | (z == length - 1)
    quad, quad_x = mine + x, theirs + 1 - x
    quad_y, quad_far = theirs + x, mine + 1 - x
    to_x = {"groups": 1 - x}
    to_y = {"dp": z * 2 + 1 - y}
    to_core = {"layer": 1 - core}
    to_line = ({"dp": dp - 2}, {"dp": dp + 2})
    has_line = (z > 0, z < length - 1)
    to_edge = (z == 1, z == length - 2)
    starts_line = [
        [has_line[way] & ((j == x) | ~to_edge[way]) for way in range(2)]
        for j in range(2)
    ]

    get_query = pltpu.make_async_copy(query_ref.at[0], own, query_sem)
    get_query.start()

    def get_store(i):
        at = pl.ds(pl.multiple_of(i * width, width), width)
        return pltpu.make_async_copy(store_ref.at[0, :, at], raw.at[i], store_sem.at[i])

    barrier = pltpu.get_barrier_semaphore()
    for peer in (to_x, to_y, to_core):
        pl.semaphore_signal(barrier, inc=1, device_id=peer, device_id_type=MESH)
    for way in range(2):

        @pl.when(has_line[way])
        def _():
            pl.semaphore_signal(
                barrier, inc=1, device_id=to_line[way], device_id_type=MESH
            )

    part_rows = rows.shape[2] // PARTS

    def chunk_copy(shard, quarter, part, send_sem, peer):
        place = rows.at[shard, quarter, pl.ds(part * part_rows, part_rows)]
        return pltpu.make_async_remote_copy(
            src_ref=place,
            dst_ref=place,
            send_sem=send_sem,
            recv_sem=recv_sem.at[shard, quarter, part],
            device_id=peer,
            device_id_type=MESH,
        )

    def line(shard, quarter, part, way):
        send_sem = line_sem.at[shard, quarter, part, way]
        return chunk_copy(shard, quarter, part, send_sem, to_line[way])

    def plane(shard, quarter, part, axis):
        send_sem = plane_sem.at[shard, quarter, part, axis]
        return chunk_copy(shard, quarter, part, send_sem, to_y if axis else to_x)

    def arrived_part(shard, quarter, part):
        plane(shard, quarter, part, 0).wait_recv()

    def arrived(shard, quarter):
        for part in range(PARTS):
            arrived_part(shard, quarter, part)

    def sent_plane(shard, quarter, axis):
        for part in range(PARTS):
            plane(shard, quarter, part, axis).wait_send()

    def sent_line(shard, quarter, way):
        for part in range(PARTS):
            line(shard, quarter, part, way).wait_send()

    def pair(block):
        return pltpu.make_async_remote_copy(
            src_ref=acc.at[block],
            dst_ref=other.at[block],
            send_sem=pair_send.at[block],
            recv_sem=pair_recv.at[block],
            device_id=to_core,
            device_id_type=MESH,
        )

    def piece(block, quarter):
        left = jnp.concatenate(
            [rows[2 * block, quarter], rows[2 * block + 1, quarter]], axis=0
        )
        dims = (((1,), (0,)), ((), ()))
        acc[block] += lax.dot_general(
            left, high[quarter], dims, preferred_element_type=jnp.float32
        ) + lax.dot_general(
            left, low[quarter], dims, preferred_element_type=jnp.float32
        )

    def convert(i):
        get_store(i).wait()
        def body(r, _):
            at = pl.ds(pl.multiple_of(r * LANES, LANES), LANES)
            value = raw[i, at, :].T
            top = value.astype(jnp.bfloat16)
            high[i, :, at] = top
            low[i, :, at] = (value - top.astype(jnp.float32)).astype(jnp.bfloat16)
            return 0

        lax.fori_loop(0, raw.shape[1] // LANES, body, 0)

    def peak(block):
        pair(block).wait_recv()
        count = acc.shape[1]
        scores = acc[block] + other[block]
        tasks = columns[pl.ds(pl.multiple_of(block * count, count), count), :]
        tasks = jnp.concatenate([tasks] * (scores.shape[1] // LANES), axis=1)
        for t in range(TASKS):
            value = jnp.where(tasks == t, scores, -jnp.inf)
            value = jnp.max(value.reshape(count // 8, 8, scores.shape[1]), axis=0)
            best[t] = jnp.maximum(best[t], value)

    def finish(block, quarter):
        piece(block, quarter)
        pair(block).start()

    get_query.wait()
    me, mate = dp, z * 2 + 1 - y
    for i in range(QUARTERS):
        at = pl.ds(i * width, width)
        factor = rate_ref[0] * lax.rsqrt(moment_ref[:, at])
        rows[me, i] = (own[:, at] * factor).astype(jnp.bfloat16)

    waits = 3 + jnp.where(z > 0, 1, 0) + jnp.where(z < length - 1, 1, 0)
    pl.semaphore_wait(barrier, waits)

    for i in range(QUARTERS):
        get_store(i).start()

    for j in range(2):
        for part in range(PARTS):
            plane(me, theirs + j, part, 1).start()
            for way in range(2):

                @pl.when(starts_line[j][way])
                def _():
                    line(me, mine + j, part, way).start()

    for i in range(columns.shape[0] // LANES):
        at = pl.ds(i * LANES, LANES)
        columns[at, :] = jnp.broadcast_to(task_ref[:, at], (LANES, LANES)).T
    acc[...] = jnp.zeros_like(acc)
    best[...] = jnp.full_like(best, -jnp.inf)
    for j in range(2):
        for part in range(PARTS):
            arrived_part(mate, mine + j, part)
            for way in range(2):

                @pl.when(starts_line[j][way])
                def _():
                    line(mate, mine + j, part, way).start()

            plane(mate, mine + j, part, 0).start()

    def convert_all():
        def body(i, _):
            convert(i)
            return 0

        lax.fori_loop(0, QUARTERS, body, 0)

    def own_plane():
        def body(i, _):
            quarter = jnp.where(i < 2, mine + i, theirs + i - 2)

            @pl.when(i >= 2)
            def _():
                arrived(mate, quarter)

            piece(z, quarter)
            return 0

        lax.fori_loop(0, QUARTERS, body, 0)
        pair(z).start()

    def source(far, way):
        return z - far if way == 0 else z + far

    def valid(src):
        return (src >= 0) & (src < length)

    def over_ways(far, action):
        def body(way, _):
            src = z + (2 * way - 1) * far

            @pl.when(valid(src))
            def _():
                action(src)

            return 0

        lax.fori_loop(0, 2, body, 0)

    def last_piece(far):
        quarter = jnp.where(edge & (far == 1), quad_far, theirs + 1)

        def body(src):
            arrived(2 * src, quarter)
            arrived(2 * src + 1, quarter)
            finish(src, quarter)

        return body

    def edge_round():
        src = jnp.where(z == 0, 1, length - 2)
        first, second = 2 * src + y, 2 * src + 1 - y

        def spread(shard):
            for part in range(PARTS):
                arrived_part(shard, quad, part)
                plane(shard, quad, part, 0).start()
                plane(shard, quad, part, 1).start()

        spread(first)
        convert_all()
        spread(second)
        own_plane()
        for part in range(PARTS):
            arrived_part(2 * src, quad_y, part)
            plane(2 * src, quad_y, part, 0).start()
            arrived_part(2 * src + 1, quad_x, part)
            plane(2 * src + 1, quad_x, part, 1).start()
        arrived(2 * src + 1, quad_y)
        arrived(2 * src, quad_x)

        def body(i, _):
            quarter = jnp.where(i == 0, quad, jnp.where(i == 1, quad_y, quad_x))
            piece(src, quarter)
            return 0

        lax.fori_loop(0, 3, body, 0)

    def pass_on(far, side, j):
        for part in range(PARTS):
            for way in range(2):
                src = source(far, way)
                shard = 2 * src + side

                @pl.when(valid(src))
                def _():
                    arrived_part(shard, mine + j, part)

                    @pl.when(has_line[1 - way])
                    def _():
                        line(shard, mine + j, part, 1 - way).start()

                    plane(shard, mine + j, part, j).start()

    def plain_round(far):
        pass_on(far, y, 0)
        pass_on(far, y, 1)

        @pl.when(far == 1)
        def _():
            convert_all()

        @pl.when(far > 1)
        def _():
            over_ways(far - 1, last_piece(far - 1))

        pass_on(far, 1 - y, 0)
        pass_on(far, 1 - y, 1)

        @pl.when(far == 1)
        def _():
            own_plane()

        def pieces(src):
            def body(i, _):
                quarter = jnp.where(i < 2, mine + i, theirs)

                @pl.when(i == 2)
                def _():
                    arrived(2 * src, theirs)
                    arrived(2 * src + 1, theirs)

                piece(src, quarter)
                return 0

            lax.fori_loop(0, 3, body, 0)

        over_ways(far, pieces)

    def round_of(far, _):
        near_edge = edge & (far == 1)
        pl.when(near_edge)(edge_round)
        pl.when(~near_edge)(lambda: plain_round(far))

        @pl.when(far == 1)
        def _():
            peak(z)

        @pl.when(far > 1)
        def _():
            over_ways(far - 1, peak)

        return 0

    lax.fori_loop(1, length, round_of, 0)
    over_ways(length - 1, last_piece(length - 1))
    over_ways(length - 1, peak)

    for t in range(TASKS):
        out_ref[pl.ds(t, 1), :] = jnp.max(best[t], axis=0, keepdims=True)

    for j in range(2):
        sent_plane(me, theirs + j, 1)
        sent_plane(mate, mine + j, 0)
        for way in range(2):

            @pl.when(starts_line[j][way])
            def _():
                sent_line(me, mine + j, way)
                sent_line(mate, mine + j, way)

    pair(z).wait_send()

    def drain(far, _):
        for way in range(2):
            src = source(far, way)

            @pl.when(valid(src))
            def _():
                pair(src).wait_send()
                near_edge = edge & (far == 1)

                @pl.when(near_edge)
                def _():
                    for side in range(2):
                        sent_plane(2 * src + side, quad, 0)
                        sent_plane(2 * src + side, quad, 1)
                    sent_plane(2 * src, quad_y, 0)
                    sent_plane(2 * src + 1, quad_x, 1)

                @pl.when(~near_edge)
                def _():
                    for j in range(2):
                        for side in range(2):
                            shard = 2 * src + side
                            sent_plane(shard, mine + j, j)

                            @pl.when(has_line[1 - way])
                            def _():
                                sent_line(shard, mine + j, 1 - way)

        return 0

    lax.fori_loop(1, length, drain, 0)


def on_device(mesh_dp, store, queries, second_moment, layer_rate, query_task):
    length = mesh_dp // 2
    examples, depth = store.shape[1], store.shape[2]
    each = queries.shape[1]
    width = depth // QUARTERS
    dma, vmem = pltpu.SemaphoreType.DMA, pltpu.VMEM
    return pl.pallas_call(
        functools.partial(kernel, length),
        out_shape=jax.ShapeDtypeStruct((TASKS, examples), jnp.float32),
        in_specs=[
            pl.BlockSpec(memory_space=pl.ANY),
            pl.BlockSpec(memory_space=pl.ANY),
            pl.BlockSpec(memory_space=pltpu.VMEM),
            pl.BlockSpec(memory_space=pltpu.SMEM),
            pl.BlockSpec(memory_space=pltpu.VMEM),
        ],
        out_specs=pl.BlockSpec(memory_space=pltpu.VMEM),
        scratch_shapes=[
            vmem((QUARTERS, examples, width), jnp.float32),
            vmem((QUARTERS, width, examples), jnp.bfloat16),
            vmem((QUARTERS, width, examples), jnp.bfloat16),
            vmem((each, depth), jnp.float32),
            vmem((mesh_dp, QUARTERS, each, width), jnp.bfloat16),
            vmem((length, 2 * each, examples), jnp.float32),
            vmem((length, 2 * each, examples), jnp.float32),
            vmem((TASKS, 8, examples), jnp.float32),
            vmem((each * mesh_dp, LANES), jnp.int32),
            dma((QUARTERS,)),
            dma,
            dma((mesh_dp, QUARTERS, PARTS)),
            dma((mesh_dp, QUARTERS, PARTS, 2)),
            dma((mesh_dp, QUARTERS, PARTS, 2)),
            dma((length,)),
            dma((length,)),
        ],
        compiler_params=pltpu.CompilerParams(
            collective_id=0, has_side_effects=True, vmem_limit_bytes=56 * 1024 * 1024
        ),
        cost_estimate=pl.CostEstimate(
            flops=4 * each * mesh_dp * examples * depth,
            bytes_accessed=4 * (examples + each) * depth,
            transcendentals=depth,
        ),
    )(store, queries, second_moment, layer_rate, query_task.reshape(1, -1))


def solution(mesh):
    in_specs = (
        P("layer", ("groups", "dp"), None),
        P("layer", "dp", None),
        P("layer", None),
        P("layer"),
        P(),
    )
    out_specs = P(None, ("groups", "dp"))
    return jax.shard_map(
        functools.partial(on_device, mesh.shape["dp"]),
        mesh=mesh,
        in_specs=in_specs,
        out_specs=out_specs,
        check_vma=False,
    )
```

```python
import functools

import jax
import jax.numpy as jnp
from jax import lax
from jax.experimental import pallas as pl
from jax.experimental.pallas import tpu as pltpu
from jax.sharding import PartitionSpec as P

TASKS = 16
QUARTERS = 4
PARTS = 1
LANES = 128
MESH = pl.DeviceIdType.MESH


def kernel(
    length,
    store_ref,
    query_ref,
    moment_ref,
    rate_ref,
    task_ref,
    out_ref,
    raw,
    high,
    low,
    own,
    rows,
    acc,
    other,
    best,
    columns,
    store_sem,
    query_sem,
    recv_sem,
    line_sem,
    plane_sem,
    pair_send,
    pair_recv,
):
    x = lax.axis_index("groups")
    dp = lax.axis_index("dp")
    core = lax.axis_index("layer")
    z, y = dp // 2, dp % 2
    parity = (x + y) % 2
    mine, theirs = 2 * parity, 2 * (1 - parity)
    width = raw.shape[2]
    edge = (z == 0) | (z == length - 1)
    quad, quad_x = mine + x, theirs + 1 - x
    quad_y, quad_far = theirs + x, mine + 1 - x
    to_x = {"groups": 1 - x}
    to_y = {"dp": z * 2 + 1 - y}
    to_core = {"layer": 1 - core}
    to_line = ({"dp": dp - 2}, {"dp": dp + 2})
    has_line = (z > 0, z < length - 1)
    to_edge = (z == 1, z == length - 2)
    starts_line = [
        [has_line[way] & ((j == x) | ~to_edge[way]) for way in range(2)]
        for j in range(2)
    ]

    get_query = pltpu.make_async_copy(query_ref.at[0], own, query_sem)
    get_query.start()

    def get_store(i):
        at = pl.ds(pl.multiple_of(i * width, width), width)
        return pltpu.make_async_copy(store_ref.at[0, :, at], raw.at[i], store_sem.at[i])

    barrier = pltpu.get_barrier_semaphore()
    for peer in (to_x, to_y, to_core):
        pl.semaphore_signal(barrier, inc=1, device_id=peer, device_id_type=MESH)
    for way in range(2):

        @pl.when(has_line[way])
        def _():
            pl.semaphore_signal(
                barrier, inc=1, device_id=to_line[way], device_id_type=MESH
            )

    part_rows = rows.shape[2] // PARTS

    def chunk_copy(shard, quarter, part, send_sem, peer):
        place = rows.at[shard, quarter, pl.ds(part * part_rows, part_rows)]
        return pltpu.make_async_remote_copy(
            src_ref=place,
            dst_ref=place,
            send_sem=send_sem,
            recv_sem=recv_sem.at[shard, quarter, part],
            device_id=peer,
            device_id_type=MESH,
        )

    def line(shard, quarter, part, way):
        send_sem = line_sem.at[shard, quarter, part, way]
        return chunk_copy(shard, quarter, part, send_sem, to_line[way])

    def plane(shard, quarter, part, axis):
        send_sem = plane_sem.at[shard, quarter, part, axis]
        return chunk_copy(shard, quarter, part, send_sem, to_y if axis else to_x)

    def arrived_part(shard, quarter, part):
        plane(shard, quarter, part, 0).wait_recv()

    def arrived(shard, quarter):
        for part in range(PARTS):
            arrived_part(shard, quarter, part)

    def sent_plane(shard, quarter, axis):
        for part in range(PARTS):
            plane(shard, quarter, part, axis).wait_send()

    def sent_line(shard, quarter, way):
        for part in range(PARTS):
            line(shard, quarter, part, way).wait_send()

    def pair(block):
        return pltpu.make_async_remote_copy(
            src_ref=acc.at[block],
            dst_ref=other.at[block],
            send_sem=pair_send.at[block],
            recv_sem=pair_recv.at[block],
            device_id=to_core,
            device_id_type=MESH,
        )

    def piece(block, quarter):
        left = jnp.concatenate(
            [rows[2 * block, quarter], rows[2 * block + 1, quarter]], axis=0
        )
        dims = (((1,), (0,)), ((), ()))
        acc[block] += lax.dot_general(
            left, high[quarter], dims, preferred_element_type=jnp.float32
        ) + lax.dot_general(
            left, low[quarter], dims, preferred_element_type=jnp.float32
        )

    def convert(i):
        get_store(i).wait()
        def body(r, _):
            at = pl.ds(pl.multiple_of(r * LANES, LANES), LANES)
            value = raw[i, at, :].T
            top = value.astype(jnp.bfloat16)
            high[i, :, at] = top
            low[i, :, at] = (value - top.astype(jnp.float32)).astype(jnp.bfloat16)
            return 0

        lax.fori_loop(0, raw.shape[1] // LANES, body, 0)

    def peak(block):
        pair(block).wait_recv()
        count = acc.shape[1]
        scores = acc[block] + other[block]
        tasks = columns[pl.ds(pl.multiple_of(block * count, count), count), :]
        tasks = jnp.concatenate([tasks] * (scores.shape[1] // LANES), axis=1)
        for t in range(TASKS):
            value = jnp.where(tasks == t, scores, -jnp.inf)
            value = jnp.max(value.reshape(count // 8, 8, scores.shape[1]), axis=0)
            best[t] = jnp.maximum(best[t], value)

    def finish(block, quarter):
        piece(block, quarter)
        pair(block).start()

    get_query.wait()
    me, mate = dp, z * 2 + 1 - y
    for i in range(QUARTERS):
        at = pl.ds(i * width, width)
        factor = rate_ref[0] * lax.rsqrt(moment_ref[:, at])
        rows[me, i] = (own[:, at] * factor).astype(jnp.bfloat16)

    waits = 3 + jnp.where(z > 0, 1, 0) + jnp.where(z < length - 1, 1, 0)
    pl.semaphore_wait(barrier, waits)

    for i in range(QUARTERS):
        get_store(i).start()

    for j in range(2):
        for part in range(PARTS):
            plane(me, theirs + j, part, 1).start()
            for way in range(2):

                @pl.when(starts_line[j][way])
                def _():
                    line(me, mine + j, part, way).start()

    for i in range(columns.shape[0] // LANES):
        at = pl.ds(i * LANES, LANES)
        columns[at, :] = jnp.broadcast_to(task_ref[:, at], (LANES, LANES)).T
    acc[...] = jnp.zeros_like(acc)
    best[...] = jnp.full_like(best, -jnp.inf)
    for j in range(2):
        for part in range(PARTS):
            arrived_part(mate, mine + j, part)
            for way in range(2):

                @pl.when(starts_line[j][way])
                def _():
                    line(mate, mine + j, part, way).start()

            plane(mate, mine + j, part, 0).start()

    def convert_all():
        def body(i, _):
            convert(i)
            return 0

        lax.fori_loop(0, QUARTERS, body, 0)

    def own_plane():
        def body(i, _):
            quarter = jnp.where(i < 2, mine + i, theirs + i - 2)

            @pl.when(i >= 2)
            def _():
                arrived(mate, quarter)

            piece(z, quarter)
            return 0

        lax.fori_loop(0, QUARTERS, body, 0)
        pair(z).start()

    def source(far, way):
        return z - far if way == 0 else z + far

    def valid(src):
        return (src >= 0) & (src < length)

    def over_ways(far, action):
        def body(way, _):
            src = z + (2 * way - 1) * far

            @pl.when(valid(src))
            def _():
                action(src)

            return 0

        lax.fori_loop(0, 2, body, 0)

    def last_piece(far):
        quarter = jnp.where(edge & (far == 1), quad_far, theirs + 1)

        def body(src):
            arrived(2 * src, quarter)
            arrived(2 * src + 1, quarter)
            finish(src, quarter)

        return body

    def edge_round():
        src = jnp.where(z == 0, 1, length - 2)
        first, second = 2 * src + y, 2 * src + 1 - y

        def spread(shard):
            for part in range(PARTS):
                arrived_part(shard, quad, part)
                plane(shard, quad, part, 0).start()
                plane(shard, quad, part, 1).start()

        spread(first)
        convert_all()
        spread(second)
        own_plane()
        for part in range(PARTS):
            arrived_part(2 * src, quad_y, part)
            plane(2 * src, quad_y, part, 0).start()
            arrived_part(2 * src + 1, quad_x, part)
            plane(2 * src + 1, quad_x, part, 1).start()
        arrived(2 * src + 1, quad_y)
        arrived(2 * src, quad_x)

        def body(i, _):
            quarter = jnp.where(i == 0, quad, jnp.where(i == 1, quad_y, quad_x))
            piece(src, quarter)
            return 0

        lax.fori_loop(0, 3, body, 0)

    def pass_on(far, side, j):
        for part in range(PARTS):
            for way in range(2):
                src = source(far, way)
                shard = 2 * src + side

                @pl.when(valid(src))
                def _():
                    arrived_part(shard, mine + j, part)

                    @pl.when(has_line[1 - way])
                    def _():
                        line(shard, mine + j, part, 1 - way).start()

                    plane(shard, mine + j, part, j).start()

    def plain_round(far):
        pass_on(far, y, 0)
        pass_on(far, y, 1)

        @pl.when(far == 1)
        def _():
            convert_all()

        pass_on(far, 1 - y, 0)
        pass_on(far, 1 - y, 1)

        @pl.when(far > 1)
        def _():
            over_ways(far - 1, last_piece(far - 1))

        @pl.when(far == 1)
        def _():
            own_plane()

        def pieces(src):
            def body(i, _):
                quarter = jnp.where(i < 2, mine + i, theirs)

                @pl.when(i == 2)
                def _():
                    arrived(2 * src, theirs)
                    arrived(2 * src + 1, theirs)

                piece(src, quarter)
                return 0

            lax.fori_loop(0, 3, body, 0)

        over_ways(far, pieces)

    def round_of(far, _):
        near_edge = edge & (far == 1)
        pl.when(near_edge)(edge_round)
        pl.when(~near_edge)(lambda: plain_round(far))

        @pl.when(far == 1)
        def _():
            peak(z)

        @pl.when(far > 1)
        def _():
            over_ways(far - 1, peak)

        return 0

    lax.fori_loop(1, length, round_of, 0)
    over_ways(length - 1, last_piece(length - 1))
    over_ways(length - 1, peak)

    for t in range(TASKS):
        out_ref[pl.ds(t, 1), :] = jnp.max(best[t], axis=0, keepdims=True)

    for j in range(2):
        sent_plane(me, theirs + j, 1)
        sent_plane(mate, mine + j, 0)
        for way in range(2):

            @pl.when(starts_line[j][way])
            def _():
                sent_line(me, mine + j, way)
                sent_line(mate, mine + j, way)

    pair(z).wait_send()

    def drain(far, _):
        for way in range(2):
            src = source(far, way)

            @pl.when(valid(src))
            def _():
                pair(src).wait_send()
                near_edge = edge & (far == 1)

                @pl.when(near_edge)
                def _():
                    for side in range(2):
                        sent_plane(2 * src + side, quad, 0)
                        sent_plane(2 * src + side, quad, 1)
                    sent_plane(2 * src, quad_y, 0)
                    sent_plane(2 * src + 1, quad_x, 1)

                @pl.when(~near_edge)
                def _():
                    for j in range(2):
                        for side in range(2):
                            shard = 2 * src + side
                            sent_plane(shard, mine + j, j)

                            @pl.when(has_line[1 - way])
                            def _():
                                sent_line(shard, mine + j, 1 - way)

        return 0

    lax.fori_loop(1, length, drain, 0)


def on_device(mesh_dp, store, queries, second_moment, layer_rate, query_task):
    length = mesh_dp // 2
    examples, depth = store.shape[1], store.shape[2]
    each = queries.shape[1]
    width = depth // QUARTERS
    dma, vmem = pltpu.SemaphoreType.DMA, pltpu.VMEM
    return pl.pallas_call(
        functools.partial(kernel, length),
        out_shape=jax.ShapeDtypeStruct((TASKS, examples), jnp.float32),
        in_specs=[
            pl.BlockSpec(memory_space=pl.ANY),
            pl.BlockSpec(memory_space=pl.ANY),
            pl.BlockSpec(memory_space=pltpu.VMEM),
            pl.BlockSpec(memory_space=pltpu.SMEM),
            pl.BlockSpec(memory_space=pltpu.VMEM),
        ],
        out_specs=pl.BlockSpec(memory_space=pltpu.VMEM),
        scratch_shapes=[
            vmem((QUARTERS, examples, width), jnp.float32),
            vmem((QUARTERS, width, examples), jnp.bfloat16),
            vmem((QUARTERS, width, examples), jnp.bfloat16),
            vmem((each, depth), jnp.float32),
            vmem((mesh_dp, QUARTERS, each, width), jnp.bfloat16),
            vmem((length, 2 * each, examples), jnp.float32),
            vmem((length, 2 * each, examples), jnp.float32),
            vmem((TASKS, 8, examples), jnp.float32),
            vmem((each * mesh_dp, LANES), jnp.int32),
            dma((QUARTERS,)),
            dma,
            dma((mesh_dp, QUARTERS, PARTS)),
            dma((mesh_dp, QUARTERS, PARTS, 2)),
            dma((mesh_dp, QUARTERS, PARTS, 2)),
            dma((length,)),
            dma((length,)),
        ],
        compiler_params=pltpu.CompilerParams(
            collective_id=0, has_side_effects=True, vmem_limit_bytes=56 * 1024 * 1024
        ),
        cost_estimate=pl.CostEstimate(
            flops=4 * each * mesh_dp * examples * depth,
            bytes_accessed=4 * (examples + each) * depth,
            transcendentals=depth,
        ),
    )(store, queries, second_moment, layer_rate, query_task.reshape(1, -1))


def solution(mesh):
    in_specs = (
        P("layer", ("groups", "dp"), None),
        P("layer", "dp", None),
        P("layer", None),
        P("layer"),
        P(),
    )
    out_specs = P(None, ("groups", "dp"))
    return jax.shard_map(
        functools.partial(on_device, mesh.shape["dp"]),
        mesh=mesh,
        in_specs=in_specs,
        out_specs=out_specs,
        check_vma=False,
    )
```

```python
import functools

import jax
import jax.numpy as jnp
from jax import lax
from jax.experimental import pallas as pl
from jax.experimental.pallas import tpu as pltpu
from jax.sharding import PartitionSpec as P

TASKS = 16
QUARTERS = 4
PARTS = 1
LANES = 128
MESH = pl.DeviceIdType.MESH


def kernel(
    length,
    store_ref,
    query_ref,
    moment_ref,
    rate_ref,
    task_ref,
    out_ref,
    raw,
    high,
    low,
    own,
    rows,
    acc,
    other,
    best,
    columns,
    store_sem,
    query_sem,
    recv_sem,
    line_sem,
    plane_sem,
    pair_send,
    pair_recv,
):
    x = lax.axis_index("groups")
    dp = lax.axis_index("dp")
    core = lax.axis_index("layer")
    z, y = dp // 2, dp % 2
    parity = (x + y) % 2
    mine, theirs = 2 * parity, 2 * (1 - parity)
    width = raw.shape[2]
    edge = (z == 0) | (z == length - 1)
    quad, quad_x = mine + x, theirs + 1 - x
    quad_y, quad_far = theirs + x, mine + 1 - x
    to_x = {"groups": 1 - x}
    to_y = {"dp": z * 2 + 1 - y}
    to_core = {"layer": 1 - core}
    to_line = ({"dp": dp - 2}, {"dp": dp + 2})
    has_line = (z > 0, z < length - 1)
    to_edge = (z == 1, z == length - 2)
    starts_line = [
        [has_line[way] & ((j == x) | ~to_edge[way]) for way in range(2)]
        for j in range(2)
    ]

    get_query = pltpu.make_async_copy(query_ref.at[0], own, query_sem)
    get_query.start()

    def get_store(i):
        at = pl.ds(pl.multiple_of(i * width, width), width)
        return pltpu.make_async_copy(store_ref.at[0, :, at], raw.at[i], store_sem.at[i])

    barrier = pltpu.get_barrier_semaphore()
    for peer in (to_x, to_y, to_core):
        pl.semaphore_signal(barrier, inc=1, device_id=peer, device_id_type=MESH)
    for way in range(2):

        @pl.when(has_line[way])
        def _():
            pl.semaphore_signal(
                barrier, inc=1, device_id=to_line[way], device_id_type=MESH
            )

    part_rows = rows.shape[2] // PARTS

    def chunk_copy(shard, quarter, part, send_sem, peer):
        place = rows.at[shard, quarter, pl.ds(part * part_rows, part_rows)]
        return pltpu.make_async_remote_copy(
            src_ref=place,
            dst_ref=place,
            send_sem=send_sem,
            recv_sem=recv_sem.at[shard, quarter, part],
            device_id=peer,
            device_id_type=MESH,
        )

    def line(shard, quarter, part, way):
        send_sem = line_sem.at[shard, quarter, part, way]
        return chunk_copy(shard, quarter, part, send_sem, to_line[way])

    def plane(shard, quarter, part, axis):
        send_sem = plane_sem.at[shard, quarter, part, axis]
        return chunk_copy(shard, quarter, part, send_sem, to_y if axis else to_x)

    def arrived_part(shard, quarter, part):
        plane(shard, quarter, part, 0).wait_recv()

    def arrived(shard, quarter):
        for part in range(PARTS):
            arrived_part(shard, quarter, part)

    def sent_plane(shard, quarter, axis):
        for part in range(PARTS):
            plane(shard, quarter, part, axis).wait_send()

    def sent_line(shard, quarter, way):
        for part in range(PARTS):
            line(shard, quarter, part, way).wait_send()

    def pair(block):
        return pltpu.make_async_remote_copy(
            src_ref=acc.at[block],
            dst_ref=other.at[block],
            send_sem=pair_send.at[block],
            recv_sem=pair_recv.at[block],
            device_id=to_core,
            device_id_type=MESH,
        )

    def piece(block, quarter):
        left = jnp.concatenate(
            [rows[2 * block, quarter], rows[2 * block + 1, quarter]], axis=0
        )
        dims = (((1,), (0,)), ((), ()))
        acc[block] += lax.dot_general(
            left, high[quarter], dims, preferred_element_type=jnp.float32
        ) + lax.dot_general(
            left, low[quarter], dims, preferred_element_type=jnp.float32
        )

    def convert(i):
        get_store(i).wait()
        def body(r, _):
            at = pl.ds(pl.multiple_of(r * LANES, LANES), LANES)
            value = raw[i, at, :].T
            top = value.astype(jnp.bfloat16)
            high[i, :, at] = top
            low[i, :, at] = (value - top.astype(jnp.float32)).astype(jnp.bfloat16)
            return 0

        lax.fori_loop(0, raw.shape[1] // LANES, body, 0)

    def peak(block):
        pair(block).wait_recv()
        count = acc.shape[1]
        scores = acc[block] + other[block]
        tasks = columns[pl.ds(pl.multiple_of(block * count, count), count), :]
        tasks = jnp.concatenate([tasks] * (scores.shape[1] // LANES), axis=1)
        for t in range(TASKS):
            value = jnp.where(tasks == t, scores, -jnp.inf)
            value = jnp.max(value.reshape(count // 8, 8, scores.shape[1]), axis=0)
            best[t] = jnp.maximum(best[t], value)

    def finish(block, quarter):
        piece(block, quarter)
        pair(block).start()

    get_query.wait()
    me, mate = dp, z * 2 + 1 - y
    for i in range(QUARTERS):
        at = pl.ds(i * width, width)
        factor = rate_ref[0] * lax.rsqrt(moment_ref[:, at])
        rows[me, i] = (own[:, at] * factor).astype(jnp.bfloat16)

    waits = 3 + jnp.where(z > 0, 1, 0) + jnp.where(z < length - 1, 1, 0)
    pl.semaphore_wait(barrier, waits)

    for i in range(QUARTERS):
        get_store(i).start()

    for j in range(2):
        for part in range(PARTS):
            plane(me, theirs + j, part, 1).start()
            for way in range(2):

                @pl.when(starts_line[j][way])
                def _():
                    line(me, mine + j, part, way).start()

    for i in range(columns.shape[0] // LANES):
        at = pl.ds(i * LANES, LANES)
        columns[at, :] = jnp.broadcast_to(task_ref[:, at], (LANES, LANES)).T
    acc[...] = jnp.zeros_like(acc)
    best[...] = jnp.full_like(best, -jnp.inf)
    for j in range(2):
        for part in range(PARTS):
            arrived_part(mate, mine + j, part)
            for way in range(2):

                @pl.when(starts_line[j][way])
                def _():
                    line(mate, mine + j, part, way).start()

            plane(mate, mine + j, part, 0).start()

    def convert_all():
        def body(i, _):
            convert(i)
            return 0

        lax.fori_loop(0, QUARTERS, body, 0)

    def own_plane():
        def body(i, _):
            quarter = jnp.where(i < 2, mine + i, theirs + i - 2)

            @pl.when(i >= 2)
            def _():
                arrived(mate, quarter)

            piece(z, quarter)
            return 0

        lax.fori_loop(0, QUARTERS, body, 0)
        pair(z).start()

    def source(far, way):
        return z - far if way == 0 else z + far

    def valid(src):
        return (src >= 0) & (src < length)

    def over_ways(far, action):
        def body(way, _):
            src = z + (2 * way - 1) * far

            @pl.when(valid(src))
            def _():
                action(src)

            return 0

        lax.fori_loop(0, 2, body, 0)

    def last_piece(far):
        quarter = jnp.where(edge & (far == 1), quad_far, theirs + 1)

        def body(src):
            arrived(2 * src, quarter)
            arrived(2 * src + 1, quarter)
            finish(src, quarter)

        return body

    def edge_round():
        src = jnp.where(z == 0, 1, length - 2)
        first, second = 2 * src + y, 2 * src + 1 - y

        def spread(shard):
            for part in range(PARTS):
                arrived_part(shard, quad, part)
                plane(shard, quad, part, 0).start()
                plane(shard, quad, part, 1).start()

        spread(first)
        convert_all()
        spread(second)
        own_plane()
        for part in range(PARTS):
            arrived_part(2 * src, quad_y, part)
            plane(2 * src, quad_y, part, 0).start()
            arrived_part(2 * src + 1, quad_x, part)
            plane(2 * src + 1, quad_x, part, 1).start()
        arrived(2 * src + 1, quad_y)
        arrived(2 * src, quad_x)

        def body(i, _):
            quarter = jnp.where(i == 0, quad, jnp.where(i == 1, quad_y, quad_x))
            piece(src, quarter)
            return 0

        lax.fori_loop(0, 3, body, 0)

    def pass_on(far, side, j):
        for part in range(PARTS):
            for way in range(2):
                src = source(far, way)
                shard = 2 * src + side

                @pl.when(valid(src))
                def _():
                    arrived_part(shard, mine + j, part)

                    @pl.when(has_line[1 - way])
                    def _():
                        line(shard, mine + j, part, 1 - way).start()

                    plane(shard, mine + j, part, j).start()

    def plain_round(far):
        pass_on(far, y, 0)
        pass_on(far, y, 1)

        @pl.when(far == 1)
        def _():
            convert_all()

        @pl.when((far > 1) & (far == length - 1))
        def _():
            over_ways(far - 1, last_piece(far - 1))

        pass_on(far, 1 - y, 0)
        pass_on(far, 1 - y, 1)

        @pl.when((far > 1) & (far < length - 1))
        def _():
            over_ways(far - 1, last_piece(far - 1))

        @pl.when(far == 1)
        def _():
            own_plane()

        def pieces(src):
            def body(i, _):
                quarter = jnp.where(i < 2, mine + i, theirs)

                @pl.when(i == 2)
                def _():
                    arrived(2 * src, theirs)
                    arrived(2 * src + 1, theirs)

                piece(src, quarter)
                return 0

            lax.fori_loop(0, 3, body, 0)

        over_ways(far, pieces)

    def round_of(far, _):
        near_edge = edge & (far == 1)
        pl.when(near_edge)(edge_round)
        pl.when(~near_edge)(lambda: plain_round(far))

        @pl.when(far == 1)
        def _():
            peak(z)

        @pl.when(far > 1)
        def _():
            over_ways(far - 1, peak)

        return 0

    lax.fori_loop(1, length, round_of, 0)
    over_ways(length - 1, last_piece(length - 1))
    over_ways(length - 1, peak)

    for t in range(TASKS):
        out_ref[pl.ds(t, 1), :] = jnp.max(best[t], axis=0, keepdims=True)

    for j in range(2):
        sent_plane(me, theirs + j, 1)
        sent_plane(mate, mine + j, 0)
        for way in range(2):

            @pl.when(starts_line[j][way])
            def _():
                sent_line(me, mine + j, way)
                sent_line(mate, mine + j, way)

    pair(z).wait_send()

    def drain(far, _):
        for way in range(2):
            src = source(far, way)

            @pl.when(valid(src))
            def _():
                pair(src).wait_send()
                near_edge = edge & (far == 1)

                @pl.when(near_edge)
                def _():
                    for side in range(2):
                        sent_plane(2 * src + side, quad, 0)
                        sent_plane(2 * src + side, quad, 1)
                    sent_plane(2 * src, quad_y, 0)
                    sent_plane(2 * src + 1, quad_x, 1)

                @pl.when(~near_edge)
                def _():
                    for j in range(2):
                        for side in range(2):
                            shard = 2 * src + side
                            sent_plane(shard, mine + j, j)

                            @pl.when(has_line[1 - way])
                            def _():
                                sent_line(shard, mine + j, 1 - way)

        return 0

    lax.fori_loop(1, length, drain, 0)


def on_device(mesh_dp, store, queries, second_moment, layer_rate, query_task):
    length = mesh_dp // 2
    examples, depth = store.shape[1], store.shape[2]
    each = queries.shape[1]
    width = depth // QUARTERS
    dma, vmem = pltpu.SemaphoreType.DMA, pltpu.VMEM
    return pl.pallas_call(
        functools.partial(kernel, length),
        out_shape=jax.ShapeDtypeStruct((TASKS, examples), jnp.float32),
        in_specs=[
            pl.BlockSpec(memory_space=pl.ANY),
            pl.BlockSpec(memory_space=pl.ANY),
            pl.BlockSpec(memory_space=pltpu.VMEM),
            pl.BlockSpec(memory_space=pltpu.SMEM),
            pl.BlockSpec(memory_space=pltpu.VMEM),
        ],
        out_specs=pl.BlockSpec(memory_space=pltpu.VMEM),
        scratch_shapes=[
            vmem((QUARTERS, examples, width), jnp.float32),
            vmem((QUARTERS, width, examples), jnp.bfloat16),
            vmem((QUARTERS, width, examples), jnp.bfloat16),
            vmem((each, depth), jnp.float32),
            vmem((mesh_dp, QUARTERS, each, width), jnp.bfloat16),
            vmem((length, 2 * each, examples), jnp.float32),
            vmem((length, 2 * each, examples), jnp.float32),
            vmem((TASKS, 8, examples), jnp.float32),
            vmem((each * mesh_dp, LANES), jnp.int32),
            dma((QUARTERS,)),
            dma,
            dma((mesh_dp, QUARTERS, PARTS)),
            dma((mesh_dp, QUARTERS, PARTS, 2)),
            dma((mesh_dp, QUARTERS, PARTS, 2)),
            dma((length,)),
            dma((length,)),
        ],
        compiler_params=pltpu.CompilerParams(
            collective_id=0, has_side_effects=True, vmem_limit_bytes=56 * 1024 * 1024
        ),
        cost_estimate=pl.CostEstimate(
            flops=4 * each * mesh_dp * examples * depth,
            bytes_accessed=4 * (examples + each) * depth,
            transcendentals=depth,
        ),
    )(store, queries, second_moment, layer_rate, query_task.reshape(1, -1))


def solution(mesh):
    in_specs = (
        P("layer", ("groups", "dp"), None),
        P("layer", "dp", None),
        P("layer", None),
        P("layer"),
        P(),
    )
    out_specs = P(None, ("groups", "dp"))
    return jax.shard_map(
        functools.partial(on_device, mesh.shape["dp"]),
        mesh=mesh,
        in_specs=in_specs,
        out_specs=out_specs,
        check_vma=False,
    )
```
